256 devices in a mesh: ind: 32 (over y, x, core), snp: 8 (over z).
Axes of the slice: x: 4, y: 4, z: 8, core: 2. Of those that a mesh axis runs over, the one named last changes fastest.
Arguments:
- genotypes: int32 [65536, 4096], P('ind', 'snp'), may hold values from 0 to 2, as said below
- targets: float32 [65536, 32], P('ind'), may hold values from -16 to 16
- ridge: float32 [1], replicated, may hold values from 0.5 to 2
- held_out: int32 [32], replicated, may hold values from 0 to 65535
Outputs:
- solution: float32 [65536, 32], P('ind')
- held_values: float32 [32], replicated
The draws below stay inside these ranges and needn't reach their ends.
Inputs may be any that keep to these rules, and one draw needn't show every extreme that they name: `held_out`: row indices of individuals. `genotypes`: each entry counts copies of one allele.
All inputs are finite; a program needn't handle non-finite values.
Results may differ from the reference program's by a relative error of at most 0.0003.
Values sent between devices are 32-bit elements; how exact they have to be, the bound alone decides.
No kernel may reach another device: no remote copies, remote signals or barrier semaphores. Data moves between devices by JAX's collectives and lax.ppermute only.
A program may use at most 64 MiB of HBM per device.

```python
import math
import jax
import jax.numpy as jnp
from jax import lax

SNPS = 4096
RHS = 32
ITERS = 4
INDIV = 65536


def genotype_codes(key):
    block_extent = min(64, SNPS // 8)
    number_of_blocks = SNPS // block_extent
    ancestor_animals = 8
    populations = 4
    random_key_list = jax.random.split(key, 8)
    population = jax.random.randint(random_key_list[0], (INDIV,), 0, populations)
    weights = jax.random.randint(random_key_list[1], (populations, number_of_blocks, ancestor_animals), 1, 9)
    cumulative = jnp.cumsum(weights, axis=2)
    frequency = jax.random.randint(random_key_list[2], (number_of_blocks, 1, block_extent), 10, 91)
    ancestor_unprocessed = (jax.random.randint(random_key_list[3], (number_of_blocks, ancestor_animals, block_extent), 0, 100) < frequency).astype(jnp.int32)
    allele_bearer = jax.random.randint(random_key_list[4], (number_of_blocks, 1, block_extent), 0, ancestor_animals)
    mating_mate = (allele_bearer + 1 + jax.random.randint(random_key_list[5], (number_of_blocks, 1, block_extent), 0, ancestor_animals - 1)) % ancestor_animals
    ancestor_identifiers = lax.broadcasted_iota(jnp.int32, (number_of_blocks, ancestor_animals, block_extent), 1)
    ancestor_alleles = jnp.where(ancestor_identifiers == allele_bearer, 1, jnp.where(ancestor_identifiers == mating_mate, 0, ancestor_unprocessed))
    mutation = jnp.power(2, jax.random.randint(random_key_list[6], (number_of_blocks,), 0, 8))

    def one_block(block_index):
        block_key = jax.random.fold_in(random_key_list[7], block_index)
        pick_key, flip_key = jax.random.split(block_key)
        bounds = cumulative[:, block_index, :][population]
        totals = bounds[:, ancestor_animals - 1:]
        picked = jax.random.randint(pick_key, (INDIV, 2), 0, totals)
        haplotypes = jnp.sum((picked[:, :, None] >= bounds[:, None, :]).astype(jnp.int32), axis=2)
        alleles = ancestor_alleles[block_index][haplotypes]
        flipped = (jax.random.randint(flip_key, (INDIV, 2, block_extent), 0, 1000) < mutation[block_index]).astype(jnp.int32)
        return jnp.sum(jnp.abs(alleles - flipped), axis=1)
    blocks_codes = lax.map(one_block, jnp.arange(number_of_blocks, dtype=jnp.int32))
    return jnp.transpose(blocks_codes, (1, 0, 2)).reshape(INDIV, SNPS).astype(jnp.int32)


def draw_genotypes(key, part):
    return genotype_codes(key)


def draw_targets(key, part):
    codes = genotype_codes(key)
    key = jax.random.fold_in(key, 11)
    effect_key, noise_key = jax.random.split(key, 2)
    column_sums = jnp.sum(codes, axis=0).astype(jnp.float32)
    square_sums = jnp.sum(codes * codes, axis=0).astype(jnp.float32)
    average = column_sums / INDIV
    inverse_sd = 1.0 / jnp.sqrt(square_sums / INDIV - average * average + 1e-05)
    standard = (codes.astype(jnp.float32) - average) * inverse_sd
    effects = jax.random.normal(effect_key, (SNPS, RHS), jnp.float32)
    noise = jax.random.normal(noise_key, (INDIV, RHS), jnp.float32)
    genetic = jnp.dot(standard, effects, precision=lax.Precision.HIGHEST, preferred_element_type=jnp.float32) / math.sqrt(SNPS)
    return jnp.clip(2.0 * genetic + 0.2 * noise, -16.0, 16.0).astype(jnp.float32)


def set_ends(values, own_key, low, high):
    spot = [jax.random.randint(jax.random.fold_in(own_key, axis), (), 0, length) for axis, length in enumerate(values.shape)]
    widest = values.shape.index(max(values.shape))
    neighbour = spot[:widest] + [(spot[widest] + 1) % values.shape[widest]] + spot[widest + 1:]
    return values.at[tuple(spot)].set(low).at[tuple(neighbour)].set(high)


def setup_inputs(seed: int = 0) -> dict:
    key_of = jax.random.split(jax.random.key(seed), 5)
    return {
        "genotypes": draw_genotypes(jax.random.fold_in(key_of[4], 71), 0),
        "targets": draw_targets(jax.random.fold_in(key_of[4], 71), 0),
        "ridge": jnp.clip(jnp.exp(jax.random.uniform(key_of[2], (1,), jnp.float32, math.log(0.5), math.log(2.0))), 0.5, 2.0),
        "held_out": set_ends(jax.random.randint(key_of[3], (RHS,), 0, INDIV), jax.random.fold_in(key_of[3], 1), 0, INDIV - 1).astype(jnp.int32),
    }


def chol_solve(gram, right):
    lower = jnp.linalg.cholesky(gram)
    inner = lax.linalg.triangular_solve(lower, right, left_side=True, lower=True)
    return lax.linalg.triangular_solve(lower, inner, left_side=True, lower=True, transpose_a=True)

def matmul(left, right):
    return jnp.dot(left.astype(jnp.float32), right.astype(jnp.float32), precision=lax.Precision.HIGHEST, preferred_element_type=jnp.float32)

def symmetric(matrix):
    return 0.5 * (matrix + matrix.T)

def reference(genotypes, targets, ridge, held_out):
    values = genotypes.astype(jnp.float32)
    mean = lax.optimization_barrier(jnp.sum(values, axis=0)) / INDIV
    second = lax.optimization_barrier(jnp.sum(values * values, axis=0)) / INDIV
    scale = 1.0 / jnp.sqrt(second - mean * mean + 1e-05)
    zmat = (values - mean) * scale

    def operate(block):
        panel = matmul(zmat.T, block)
        return matmul(zmat, panel) / SNPS + ridge[0] * block
    solution = jnp.zeros_like(targets)
    resid = targets
    direction = targets
    norm_now = symmetric(matmul(resid.T, resid))
    for step in range(ITERS):
        image = operate(direction)
        curvature = symmetric(matmul(direction.T, image))
        alpha = chol_solve(curvature, norm_now)
        solution = solution + matmul(direction, alpha)
        resid = resid - matmul(image, alpha)
        norm_next = symmetric(matmul(resid.T, resid))
        beta = chol_solve(norm_now, norm_next)
        direction = resid + matmul(direction, beta)
        norm_now = norm_next
    columns = jnp.arange(RHS, dtype=jnp.int32)
    held_values = solution[held_out, columns]
    return (solution, held_values)
```

```python
import functools

import jax
import jax.numpy as jnp
from jax import lax
from jax.experimental import pallas as pl
from jax.experimental.pallas import tpu as pltpu
from jax.sharding import PartitionSpec as P

ITERS = 4
RHS = 32
XSIZE, YSIZE, CORES = 4, 4, 2
F32, BF16 = jnp.float32, jnp.bfloat16
NT = (((1,), (1,)), ((), ()))
PARAMS = pltpu.CompilerParams(vmem_limit_bytes=40 * 1024 * 1024)


def split(x):
    high = x.astype(BF16)
    rest = x - high.astype(F32)
    mid = rest.astype(BF16)
    low = (rest - mid.astype(F32)).astype(BF16)
    return high, mid, low


def stacked(x):
    return jnp.concatenate(split(x), axis=0)


def fold(x):
    n = x.shape[0] // 3
    return x[:n] + (x[n:2 * n] + x[2 * n:])


def gram(left, right):
    full = fold(lax.dot_general(left, right, NT, preferred_element_type=F32))
    n = full.shape[1] // 3
    return full[:, :n] + (full[:, n:2 * n] + full[:, 2 * n:])


def small_dot(left, right):
    lh, lm, ll = split(left)
    rh, rm, rl = split(right)
    lhs = jnp.concatenate([lh, lh, lm, lm, lh, ll], axis=1)
    rhs = jnp.concatenate([rh, rm, rh, rm, rl, rh], axis=0)
    return jnp.dot(lhs, rhs, preferred_element_type=F32)


def symmetric(x):
    return 0.5 * (x + x.T)


def right_divide(gram_, top):
    n = gram_.shape[0]
    m = jnp.concatenate([gram_, top], axis=0)
    lane = lax.broadcasted_iota(jnp.int32, m.shape, 1)
    for k in range(n):
        row = m[k:k + 1, :]
        col = m[:, k:k + 1] * (1.0 / m[k:k + 1, k:k + 1])
        m = jnp.where(lane == k, col, m - col * row)
    return m[n:]


def prep_kernel(geno_ref, rhs_ref, codes_ref, pay_ref, all_ref):
    step = pl.program_id(0)
    rows, cols = geno_ref.shape
    centred = (geno_ref[...] - 1).astype(F32)
    codes = centred.astype(BF16)
    codes_ref[...] = codes
    all_ref[pl.ds(pl.multiple_of(step * rows, rows), rows), :] = codes
    squares = jnp.sum(centred * centred, axis=0, keepdims=True)

    @pl.when(step == 0)
    def _():
        pay_ref[...] = jnp.zeros_like(pay_ref)
        pay_ref[33:34, :cols] = squares

    @pl.when(step > 0)
    def _():
        pay_ref[33:34, :cols] += squares

    @pl.when(step == pl.num_programs(0) - 1)
    def _():
        rhs = rhs_ref[...]
        pieces = stacked(rhs)
        lhs = jnp.concatenate([pieces, jnp.ones((32, pieces.shape[1]), BF16)], axis=0)
        acc = jnp.dot(lhs, all_ref[...], preferred_element_type=F32)
        pay_ref[0:RHS, :cols] = fold(acc[:96])
        pay_ref[32:33, :cols] = acc[96:97]
        pay_ref[0:RHS, cols:cols + 32] = gram(pieces, pieces)
        pay_ref[0:RHS, cols + 32:cols + 33] = jnp.sum(rhs, axis=1, keepdims=True)


def prep(genotypes, rhs):
    rows, cols = genotypes.shape
    block = 256
    return pl.pallas_call(
        prep_kernel,
        grid=(rows // block,),
        in_specs=[pl.BlockSpec((block, cols), lambda i: (i, 0)), pl.BlockSpec((RHS, rows), lambda i: (0, 0))],
        out_specs=[pl.BlockSpec((block, cols), lambda i: (i, 0)), pl.BlockSpec((40, cols + 128), lambda i: (0, 0))],
        out_shape=[jax.ShapeDtypeStruct((rows, cols), BF16), jax.ShapeDtypeStruct((40, cols + 128), F32)],
        scratch_shapes=[pltpu.VMEM((rows, cols), BF16)],
        compiler_params=PARAMS,
        name="prep",
    )(genotypes, rhs)


def panel_kernel(total, first, last, parts, *refs):
    if first:
        red_ref, codes_ref, resid_ref, u_ref, stat_ref, norm_ref, pp_ref, dir_ref, out_ref = refs
    else:
        (red_ref, codes_ref, resid_ref, olddir_ref, oldu_ref, stat_in_ref, inv_ref, oldpp_ref,
         u_ref, norm_ref, pp_ref, dir_ref, beta_ref, out_ref) = refs
    cols = codes_ref.shape[1]
    if first:
        mean = red_ref[32:33, :cols] * (1.0 / total)
        scale = 1.0 / jnp.sqrt(red_ref[33:34, :cols] * (1.0 / total) - mean * mean + 1e-05)
        stat_ref[0:1, :] = mean
        stat_ref[1:2, :] = scale
    else:
        mean, scale = stat_in_ref[0:1, :], stat_in_ref[1:2, :]
    side = red_ref[0:RHS, cols:cols + 128]
    norm = symmetric(side[:, :32])
    u = (red_ref[0:RHS, :cols] - side[:, 32:33] * mean) * scale
    norm_ref[...] = norm
    if first:
        pp = norm
        dir_ref[...] = resid_ref[...]
    else:
        beta = small_dot(norm, inv_ref[...])
        u = u + small_dot(beta, oldu_ref[...])
        cross = small_dot(beta, side[:, 64:96])
        pp = norm + (cross + cross.T) + symmetric(small_dot(small_dot(beta, oldpp_ref[...]), beta.T))
        dir_ref[...] = resid_ref[...] + small_dot(beta, olddir_ref[...])
        beta_ref[...] = beta
    pp_ref[...] = pp
    u_ref[...] = u
    pieces = stacked(u)
    uu = gram(pieces, pieces)
    if last:
        for j in range(parts):
            out_ref[j, :, :] = jnp.zeros(out_ref.shape[1:], F32)
            out_ref[j, :, 0:32] = uu
        return
    weight = u * scale
    image = fold(lax.dot_general(stacked(weight), codes_ref[...], NT, preferred_element_type=F32))
    image = image - jnp.sum(weight * mean, axis=1, keepdims=True)
    width = image.shape[1] // parts
    for j in range(parts):
        out_ref[j, :, 0:width] = image[:, j * width:(j + 1) * width]
        out_ref[j, :, width:] = jnp.zeros((RHS, 128), F32)
        out_ref[j, :, width:width + 32] = uu


def panel(total, first, last, parts, *args):
    rows, cols = args[1].shape
    small = jax.ShapeDtypeStruct((RHS, RHS), F32)
    outs = [jax.ShapeDtypeStruct((RHS, cols), F32)]
    if first:
        outs.append(jax.ShapeDtypeStruct((8, cols), F32))
    outs += [small, small, jax.ShapeDtypeStruct((RHS, rows), F32)]
    if not first:
        outs.append(small)
    outs.append(jax.ShapeDtypeStruct((parts, RHS, (0 if last else rows // parts) + 128), F32))
    return pl.pallas_call(
        functools.partial(panel_kernel, total, first, last, parts),
        out_shape=outs,
        compiler_params=PARAMS,
        name="panel",
    )(*args)


def step_kernel(markers, first, held_too, *refs):
    it = iter(refs)
    ridge_ref, image_ref, uu_ref, pp_ref, norm_ref, resid_ref, dir_ref = [next(it) for _ in range(7)]
    sol_in = None if first else next(it)
    codes_ref = next(it)
    held_ref = next(it) if held_too else None
    sol_ref, newres_ref, inv_ref, pay_ref = [next(it) for _ in range(4)]
    cols = codes_ref.shape[1]
    lam = ridge_ref[0]
    norm = norm_ref[...]
    eye = (lax.broadcasted_iota(jnp.int32, norm.shape, 0) == lax.broadcasted_iota(jnp.int32, norm.shape, 1)).astype(F32)
    alpha = right_divide(symmetric(uu_ref[...] * (1.0 / markers) + lam * pp_ref[...]), norm)
    inv_ref[...] = right_divide(norm, eye)
    direction = dir_ref[...]
    image = jnp.concatenate([image_ref[j] for j in range(image_ref.shape[0])], axis=1)
    image = image * (1.0 / markers) + lam * direction
    resid = resid_ref[...] - small_dot(alpha, image)
    sol = small_dot(alpha, direction)
    if not first:
        sol = sol_in[...] + sol
    sol_ref[...] = sol
    newres_ref[...] = resid
    pieces = stacked(resid)
    dpieces = stacked(direction)
    pay_ref[:, :cols] = fold(jnp.dot(pieces, codes_ref[...], preferred_element_type=F32))
    pay_ref[:, cols:] = jnp.zeros((RHS, pay_ref.shape[1] - cols), F32)
    pay_ref[:, cols:cols + 32] = gram(pieces, pieces)
    pay_ref[:, cols + 32:cols + 33] = jnp.sum(resid, axis=1, keepdims=True)
    pay_ref[:, cols + 64:cols + 96] = gram(dpieces, pieces)
    if held_too:
        place = lax.broadcasted_iota(jnp.int32, resid.shape, 1)
        chosen = (place == held_ref[...]).astype(BF16)
        pay_ref[:, cols + 128:cols + 160] = fold(lax.dot_general(pieces, chosen, NT, preferred_element_type=F32))
        pay_ref[:, cols + 160:cols + 192] = fold(lax.dot_general(dpieces, chosen, NT, preferred_element_type=F32))
        pay_ref[:, cols + 192:cols + 224] = fold(lax.dot_general(stacked(sol), chosen, NT, preferred_element_type=F32))


def step(markers, first, held_too, *args):
    codes = args[-2] if held_too else args[-1]
    rows, cols = codes.shape
    vmem = pl.BlockSpec(memory_space=pltpu.VMEM)
    long = jax.ShapeDtypeStruct((RHS, rows), F32)
    return pl.pallas_call(
        functools.partial(step_kernel, markers, first, held_too),
        in_specs=[pl.BlockSpec(memory_space=pltpu.SMEM)] + [vmem] * (len(args) - 1),
        out_shape=[long, long, jax.ShapeDtypeStruct((RHS, RHS), F32),
                   jax.ShapeDtypeStruct((RHS, cols + (256 if held_too else 128)), F32)],
        compiler_params=PARAMS,
        name="step",
    )(*args)


def last_kernel(markers, cols, ridge_ref, uu_ref, pp_ref, norm_ref, dir_ref, sol_ref, red_ref, beta_ref, out_ref, held_ref):
    alpha = right_divide(symmetric(uu_ref[...] * (1.0 / markers) + ridge_ref[0] * pp_ref[...]), norm_ref[...])
    out_ref[...] = sol_ref[...] + small_dot(alpha, dir_ref[...])
    side = red_ref[:, cols + 128:cols + 256]
    direction = side[:, 0:32] + small_dot(beta_ref[...], side[:, 32:64])
    rows = side[:, 64:96] + small_dot(alpha, direction)
    eye = lax.broadcasted_iota(jnp.int32, rows.shape, 0) == lax.broadcasted_iota(jnp.int32, rows.shape, 1)
    held_ref[...] = jnp.sum(jnp.where(eye, rows, 0.0), axis=0, keepdims=True)


def last_step(markers, cols, *args):
    vmem = pl.BlockSpec(memory_space=pltpu.VMEM)
    return pl.pallas_call(
        functools.partial(last_kernel, markers, cols),
        in_specs=[pl.BlockSpec(memory_space=pltpu.SMEM)] + [vmem] * (len(args) - 1),
        out_shape=[jax.ShapeDtypeStruct(args[4].shape, F32), jax.ShapeDtypeStruct((1, RHS), F32)],
        compiler_params=PARAMS,
        name="last",
    )(*args)


def on_ind(move):
    pairs = []
    for y in range(YSIZE):
        for x in range(XSIZE):
            for c in range(CORES):
                ty, tx, tc = move(y, x, c)
                pairs.append(((y * XSIZE + x) * CORES + c, (ty * XSIZE + tx) * CORES + tc))
    return pairs


def sum_ind(value):
    for along in ("x", "y"):
        moved = []
        for d in (1, 2, 3):
            if along == "x":
                pairs = on_ind(lambda y, x, c, d=d: (y, (x + d) % XSIZE, c))
            else:
                pairs = on_ind(lambda y, x, c, d=d: ((y + d) % YSIZE, x, c))
            moved.append(lax.ppermute(value, "ind", pairs))
        value = (value + moved[1]) + (moved[0] + moved[2])
    return value + lax.ppermute(value, "ind", on_ind(lambda y, x, c: (y, x, 1 - c)))


def exchange(value):
    return lax.all_to_all(value, "snp", 0, 0)


def shards(genotypes, targets, ridge, held_out):
    rows, cols = genotypes.shape
    parts = lax.axis_size("snp")
    total = rows * lax.axis_size("ind")
    markers = cols * parts
    width = rows // parts
    place = (held_out - lax.axis_index("ind") * rows)[:, None]

    resid = targets.T
    codes, pay = prep(genotypes, resid)
    sol = None
    for k in range(ITERS):
        first, last = k == 0, k == ITERS - 1
        red = sum_ind(pay)
        if first:
            u, stat, norm, pp, direction, out = panel(total, True, False, parts, red, codes, resid)
        else:
            u, norm, pp, direction, beta, out = panel(
                total, False, last, parts, red, codes, resid, direction, u, stat, inv, pp)
        got = jnp.sum(exchange(out), axis=0)
        if last:
            break
        uu = got[:, width:width + RHS]
        image = exchange(jnp.broadcast_to(got[None, :, :width], (parts, RHS, width)))
        args = [ridge, image, uu, pp, norm, resid, direction]
        if not first:
            args.append(sol)
        args.append(codes)
        held_too = k == ITERS - 2
        if held_too:
            args.append(place)
        sol, resid, inv, pay = step(markers, first, held_too, *args)
    sol, held = last_step(markers, cols, ridge, got[:, :RHS], pp, norm, direction, sol, red, beta)
    return sol.T, held[0]


def solution(mesh):
    return jax.shard_map(
        shards,
        mesh=mesh,
        in_specs=(P("ind", "snp"), P("ind", None), P(), P()),
        out_specs=(P("ind", None), P()),
        check_vma=False,
    )
```

```python
import functools

import jax
import jax.numpy as jnp
from jax import lax
from jax.experimental import pallas as pl
from jax.experimental.pallas import tpu as pltpu
from jax.sharding import PartitionSpec as P

ITERS = 4
RHS = 32
XSIZE, YSIZE, CORES = 4, 4, 2
F32, BF16 = jnp.float32, jnp.bfloat16
NT = (((1,), (1,)), ((), ()))
PARAMS = pltpu.CompilerParams(vmem_limit_bytes=12 * 1024 * 1024)


def split(x):
    high = x.astype(BF16)
    rest = x - high.astype(F32)
    mid = rest.astype(BF16)
    low = (rest - mid.astype(F32)).astype(BF16)
    return high, mid, low


def stacked(x):
    return jnp.concatenate(split(x), axis=0)


def fold(x):
    n = x.shape[0] // 3
    return x[:n] + (x[n:2 * n] + x[2 * n:])


def gram(left, right):
    full = fold(lax.dot_general(left, right, NT, preferred_element_type=F32))
    n = full.shape[1] // 3
    return full[:, :n] + (full[:, n:2 * n] + full[:, 2 * n:])


def small_dot(left, right):
    lh, lm, ll = split(left)
    rh, rm, rl = split(right)
    lhs = jnp.concatenate([lh, lh, lm, lm, lh, ll], axis=1)
    rhs = jnp.concatenate([rh, rm, rh, rm, rl, rh], axis=0)
    return jnp.dot(lhs, rhs, preferred_element_type=F32)


def symmetric(x):
    return 0.5 * (x + x.T)


def left_divide(gram_, right):
    n = gram_.shape[0]
    diag = lax.broadcasted_iota(jnp.int32, (n, n), 0) == lax.broadcasted_iota(jnp.int32, (n, n), 1)
    only = jnp.where(diag, gram_, 0.0)
    down = lax.rsqrt(jnp.sum(only, axis=1, keepdims=True))
    across = lax.rsqrt(jnp.sum(only, axis=0, keepdims=True))
    m = jnp.concatenate([gram_ * across, right], axis=1) * down
    sub = lax.broadcasted_iota(jnp.int32, (n, 1), 0)
    for k in range(0, n, 2):
        c0 = jnp.broadcast_to(m[:, k:k + 1], m.shape)
        c1 = jnp.broadcast_to(m[:, k + 1:k + 2], m.shape)
        r0, r1 = m[k:k + 1, :], m[k + 1:k + 2, :]
        p, q, r = c0[k:k + 1, :], c0[k + 1:k + 2, :], c1[k + 1:k + 2, :]
        inverse = 1.0 / (p * r - q * q)
        n0 = (r * r0 - q * r1) * inverse
        n1 = (p * r1 - q * r0) * inverse
        m = jnp.where(sub == k, n0, jnp.where(sub == k + 1, n1, m - c0 * n0 - c1 * n1))
    return m[:, n:] * down


SIDE = {"norm": (0, 0), "sums": (0, 32), "held_resid": (0, 64), "cross": (1, 0), "held_dir": (1, 32), "held_sol": (1, 64)}


def put(ref, name, value):
    half, lane = SIDE[name]
    lane += ref.shape[2] - 128
    ref[half, 0:RHS, lane:lane + value.shape[1]] = value


def take(ref, name, lanes=RHS):
    half, lane = SIDE[name]
    lane += ref.shape[2] - 128
    return ref[half, 0:RHS, lane:lane + lanes]


QUARTERS = 4


def prep_kernel(geno_hbm, rhs_hbm, codes_ref, pay_ref, geno_ref, rhs_ref, sems):
    rows, cols = geno_ref.shape
    half, chunk = cols // 2, rows // QUARTERS
    rhs_copy = pltpu.make_async_copy(rhs_hbm, rhs_ref, sems.at[QUARTERS])
    rhs_copy.start()
    copies = []
    for q in range(QUARTERS):
        part = pl.ds(q * chunk, chunk)
        copies.append(pltpu.make_async_copy(geno_hbm.at[part, :], geno_ref.at[part, :], sems.at[q]))
        copies[-1].start()
    rhs_copy.wait()
    rhs = rhs_ref[...]
    pieces = stacked(rhs)
    pay_ref[...] = jnp.zeros_like(pay_ref)
    put(pay_ref, "norm", gram(pieces, pieces))
    put(pay_ref, "sums", jnp.sum(rhs, axis=1, keepdims=True))
    lhs = jnp.concatenate([pieces, jnp.ones((32, rows), BF16)], axis=0)
    panel_, sums, squares = 0.0, 0.0, 0.0
    for q in range(QUARTERS):
        copies[q].wait()
        centred = (geno_ref[q * chunk:(q + 1) * chunk, :] - 1).astype(F32)
        codes = centred.astype(BF16)
        codes_ref[q * chunk:(q + 1) * chunk, :] = codes
        squares = squares + jnp.sum(centred * centred, axis=0, keepdims=True)
        acc = jnp.dot(lhs[:, q * chunk:(q + 1) * chunk], codes, preferred_element_type=F32)
        panel_ = panel_ + fold(acc[:96])
        sums = sums + acc[96:97]
    for c in range(2):
        part = slice(c * half, (c + 1) * half)
        pay_ref[c, 0:RHS, :half] = panel_[:, part]
        pay_ref[c, 32:33, :half] = sums[:, part]
        pay_ref[c, 33:34, :half] = squares[:, part]


def prep(genotypes, rhs):
    rows, cols = genotypes.shape
    hbm = pl.BlockSpec(memory_space=pltpu.HBM)
    return pl.pallas_call(
        prep_kernel,
        in_specs=[hbm, hbm],
        out_shape=[jax.ShapeDtypeStruct((rows, cols), BF16), jax.ShapeDtypeStruct((2, 40, cols // 2 + 128), F32)],
        scratch_shapes=[pltpu.VMEM((rows, cols), jnp.int32), pltpu.VMEM((RHS, rows), F32),
                        pltpu.SemaphoreType.DMA((QUARTERS + 1,))],
        compiler_params=PARAMS,
        name="prep",
    )(pltpu.with_memory_space_constraint(genotypes, pltpu.HBM), pltpu.with_memory_space_constraint(rhs, pltpu.HBM))


def panel_kernel(total, first, last, parts, *refs):
    if first:
        red_ref, codes_ref, u_ref, stat_ref, norm_ref, pp_ref, out_ref = refs
    else:
        red_ref, codes_ref, oldu_ref, stat_in_ref, inv_ref, oldpp_ref, u_ref, norm_ref, pp_ref, beta_ref, out_ref = refs
    half = red_ref.shape[2] - 128

    def row(i):
        return jnp.concatenate([red_ref[0, i:i + 1, :half], red_ref[1, i:i + 1, :half]], axis=1)

    if first:
        mean = row(32) * (1.0 / total)
        scale = 1.0 / jnp.sqrt(row(33) * (1.0 / total) - mean * mean + 1e-05)
        stat_ref[0:1, :] = mean
        stat_ref[1:2, :] = scale
    else:
        mean, scale = stat_in_ref[0:1, :], stat_in_ref[1:2, :]
    norm = symmetric(take(red_ref, "norm"))
    u = jnp.concatenate([red_ref[0, 0:RHS, :half], red_ref[1, 0:RHS, :half]], axis=1)
    u = (u - take(red_ref, "sums", 1) * mean) * scale
    norm_ref[...] = norm
    if first:
        pp = norm
    else:
        beta = small_dot(norm, inv_ref[...])
        u = u + small_dot(beta, oldu_ref[...])
        cross = small_dot(beta, take(red_ref, "cross"))
        pp = norm + (cross + cross.T) + symmetric(small_dot(small_dot(beta, oldpp_ref[...]), beta.T))
        beta_ref[...] = beta
    pp_ref[...] = pp
    u_ref[...] = u
    pieces = stacked(u)
    uu = gram(pieces, pieces)
    packed = jnp.concatenate([uu[4 * i:4 * i + 4] for i in range(8)], axis=1)
    if last:
        for j in range(parts):
            out_ref[j, :, :] = packed
        return
    weight = u * scale
    image = fold(lax.dot_general(stacked(weight), codes_ref[...], NT, preferred_element_type=F32))
    image = image - jnp.sum(weight * mean, axis=1, keepdims=True)
    width = image.shape[1] // parts
    for j in range(parts):
        out_ref[j, 0:RHS, :] = image[:, j * width:(j + 1) * width]
        out_ref[j, RHS:, :] = packed


def unpack(block):
    return jnp.concatenate([block[0:4, 32 * i:32 * i + 32] for i in range(8)], axis=0)


def panel(total, first, last, parts, *args):
    rows, cols = args[1].shape
    small = jax.ShapeDtypeStruct((RHS, RHS), F32)
    outs = [jax.ShapeDtypeStruct((RHS, cols), F32)]
    if first:
        outs.append(jax.ShapeDtypeStruct((8, cols), F32))
    outs += [small, small]
    if not first:
        outs.append(small)
    outs.append(jax.ShapeDtypeStruct((parts, 4 if last else RHS + 4, 256), F32))
    return pl.pallas_call(
        functools.partial(panel_kernel, total, first, last, parts),
        out_shape=outs,
        compiler_params=PARAMS,
        name="panel",
    )(*args)


def solve_kernel(markers, first, *refs):
    if first:
        ridge_ref, got_ref, pp_ref, norm_ref, resid_ref, send_ref, alpha_ref, inv_ref, sol_ref, base_ref = refs
    else:
        (ridge_ref, got_ref, pp_ref, norm_ref, resid_ref, beta_ref, olddir_ref, oldsol_ref,
         send_ref, alpha_ref, inv_ref, sol_ref, base_ref, dir_ref) = refs
    lam = ridge_ref[0]
    norm = norm_ref[...]
    parts = got_ref.shape[0]
    got = got_ref[0]
    for j in range(1, parts):
        got = got + got_ref[j]
    eye = (lax.broadcasted_iota(jnp.int32, norm.shape, 0) == lax.broadcasted_iota(jnp.int32, norm.shape, 1)).astype(F32)
    curvature = symmetric(unpack(got[RHS:]) * (1.0 / markers) + lam * pp_ref[...])
    alpha = left_divide(curvature, norm).T
    inv_ref[...] = left_divide(norm, eye)
    alpha_ref[...] = alpha * (1.0 / markers)
    for j in range(parts):
        send_ref[j, :, :] = got[:RHS]
    resid = resid_ref[...]
    if first:
        direction = resid
    else:
        direction = resid + small_dot(beta_ref[...], olddir_ref[...])
        dir_ref[...] = direction
    move = small_dot(alpha, direction)
    sol_ref[...] = move if first else oldsol_ref[...] + move
    base_ref[...] = resid - lam * move


def solve(markers, first, *args):
    vmem = pl.BlockSpec(memory_space=pltpu.VMEM)
    long = jax.ShapeDtypeStruct(args[4].shape, F32)
    small = jax.ShapeDtypeStruct((RHS, RHS), F32)
    parts, _, width = args[1].shape
    return pl.pallas_call(
        functools.partial(solve_kernel, markers, first),
        in_specs=[pl.BlockSpec(memory_space=pltpu.SMEM)] + [vmem] * (len(args) - 1),
        out_shape=[jax.ShapeDtypeStruct((parts, RHS, width), F32), small, small, long, long] + ([] if first else [long]),
        compiler_params=PARAMS,
        name="solve",
    )(*args)


def step_kernel(held_too, *refs):
    if held_too:
        image_ref, alpha_ref, base_ref, dir_ref, codes_ref, sol_ref, held_ref, resid_ref, pay_ref = refs
    else:
        image_ref, alpha_ref, base_ref, dir_ref, codes_ref, resid_ref, pay_ref = refs
    half = codes_ref.shape[1] // 2
    image = jnp.concatenate([image_ref[j] for j in range(image_ref.shape[0])], axis=1)
    resid = base_ref[...] - small_dot(alpha_ref[...], image)
    resid_ref[...] = resid
    pieces = stacked(resid)
    dpieces = stacked(dir_ref[...])
    panel_ = fold(jnp.dot(pieces, codes_ref[...], preferred_element_type=F32))
    for c in range(2):
        pay_ref[c, :, :half] = panel_[:, c * half:(c + 1) * half]
        pay_ref[c, :, half:] = jnp.zeros((RHS, 128), F32)
    put(pay_ref, "norm", gram(pieces, pieces))
    put(pay_ref, "sums", jnp.sum(resid, axis=1, keepdims=True))
    put(pay_ref, "cross", gram(dpieces, pieces))
    if held_too:
        place = lax.broadcasted_iota(jnp.int32, resid.shape, 1)
        chosen = (place == held_ref[...]).astype(BF16)
        for name, value in (("held_resid", pieces), ("held_dir", dpieces), ("held_sol", stacked(sol_ref[...]))):
            put(pay_ref, name, fold(lax.dot_general(value, chosen, NT, preferred_element_type=F32)))


def step(held_too, *args):
    rows, cols = args[4].shape
    return pl.pallas_call(
        functools.partial(step_kernel, held_too),
        out_shape=[jax.ShapeDtypeStruct((RHS, rows), F32), jax.ShapeDtypeStruct((2, RHS, cols // 2 + 128), F32)],
        compiler_params=PARAMS,
        name="step",
    )(*args)


def last_kernel(markers, ridge_ref, got_ref, pp_ref, norm_ref, beta_ref, resid_ref, olddir_ref, sol_ref, red_ref,
                out_ref, held_ref):
    got = got_ref[0]
    for j in range(1, got_ref.shape[0]):
        got = got + got_ref[j]
    alpha = left_divide(symmetric(unpack(got) * (1.0 / markers) + ridge_ref[0] * pp_ref[...]), norm_ref[...]).T
    beta = beta_ref[...]
    out_ref[...] = sol_ref[...] + small_dot(alpha, resid_ref[...] + small_dot(beta, olddir_ref[...]))
    direction = take(red_ref, "held_resid") + small_dot(beta, take(red_ref, "held_dir"))
    rows = take(red_ref, "held_sol") + small_dot(alpha, direction)
    eye = lax.broadcasted_iota(jnp.int32, rows.shape, 0) == lax.broadcasted_iota(jnp.int32, rows.shape, 1)
    held_ref[...] = jnp.sum(jnp.where(eye, rows, 0.0), axis=0, keepdims=True)


def last_step(markers, *args):
    vmem = pl.BlockSpec(memory_space=pltpu.VMEM)
    return pl.pallas_call(
        functools.partial(last_kernel, markers),
        in_specs=[pl.BlockSpec(memory_space=pltpu.SMEM)] + [vmem] * (len(args) - 1),
        out_shape=[jax.ShapeDtypeStruct(args[5].shape, F32), jax.ShapeDtypeStruct((1, RHS), F32)],
        compiler_params=PARAMS,
        name="last",
    )(*args)


def on_ind(move):
    pairs = []
    for y in range(YSIZE):
        for x in range(XSIZE):
            for c in range(CORES):
                ty, tx, tc = move(y, x, c)
                pairs.append(((y * XSIZE + x) * CORES + c, (ty * XSIZE + tx) * CORES + tc))
    return pairs


def swap_cores(value):
    return lax.ppermute(value, "ind", on_ind(lambda y, x, c: (y, x, 1 - c)))


def sum_ind(value):
    odd = lax.axis_index("ind") % CORES == 1
    mine = jnp.where(odd, value[1], value[0])
    mine = mine + swap_cores(jnp.where(odd, value[0], value[1]))
    for along in ("x", "y"):
        moved = []
        for d in (1, 2, 3):
            if along == "x":
                pairs = on_ind(lambda y, x, c, d=d: (y, (x + d) % XSIZE, c))
            else:
                pairs = on_ind(lambda y, x, c, d=d: ((y + d) % YSIZE, x, c))
            moved.append(lax.ppermute(mine, "ind", pairs))
        mine = (mine + moved[1]) + (moved[0] + moved[2])
    other = swap_cores(mine)
    return jnp.stack([jnp.where(odd, other, mine), jnp.where(odd, mine, other)])


def exchange(value):
    return lax.all_to_all(value, "snp", 0, 0)


def shards(genotypes, targets, ridge, held_out):
    rows, cols = genotypes.shape
    parts = lax.axis_size("snp")
    total = rows * lax.axis_size("ind")
    markers = cols * parts
    place = (held_out - lax.axis_index("ind") * rows)[:, None]

    resid = targets.T
    codes, pay = prep(genotypes, resid)
    for k in range(ITERS):
        first, last = k == 0, k == ITERS - 1
        red = sum_ind(pay)
        if first:
            u, stat, norm, pp, out = panel(total, True, False, parts, red, codes)
        else:
            u, norm, pp, beta, out = panel(total, False, last, parts, red, codes, u, stat, inv, pp)
        got = exchange(out)
        if last:
            break
        args = [ridge, got, pp, norm, resid]
        if first:
            direction = resid
            send, alpha, inv, sol, base = solve(markers, True, *args)
        else:
            send, alpha, inv, sol, base, direction = solve(markers, False, *args, beta, direction, sol)
        image = exchange(send)
        held_too = k == ITERS - 2
        resid, pay = step(held_too, image, alpha, base, direction, codes, *([sol, place] if held_too else []))
    sol, held = last_step(markers, ridge, got, pp, norm, beta, resid, direction, sol, red)
    return sol.T, held[0]


def solution(mesh):
    return jax.shard_map(
        shards,
        mesh=mesh,
        in_specs=(P("ind", "snp"), P("ind", None), P(), P()),
        out_specs=(P("ind", None), P()),
        check_vma=False,
    )
```

```python
import functools

import jax
import jax.numpy as jnp
from jax import lax
from jax.experimental import pallas as pl
from jax.experimental.pallas import tpu as pltpu
from jax.sharding import PartitionSpec as P

ITERS = 4
RHS = 32
XSIZE, YSIZE, CORES = 4, 4, 2
F32, BF16 = jnp.float32, jnp.bfloat16
NT = (((1,), (1,)), ((), ()))
PARAMS = pltpu.CompilerParams(vmem_limit_bytes=12 * 1024 * 1024)


def split(x):
    high = x.astype(BF16)
    rest = x - high.astype(F32)
    mid = rest.astype(BF16)
    low = (rest - mid.astype(F32)).astype(BF16)
    return high, mid, low


def stacked(x):
    return jnp.concatenate(split(x), axis=0)


def fold(x):
    n = x.shape[0] // 3
    return x[:n] + (x[n:2 * n] + x[2 * n:])


def gram(left, right):
    full = fold(lax.dot_general(left, right, NT, preferred_element_type=F32))
    n = full.shape[1] // 3
    return full[:, :n] + (full[:, n:2 * n] + full[:, 2 * n:])


def small_dot(left, right):
    lh, lm, ll = split(left)
    rh, rm, rl = split(right)
    lhs = jnp.concatenate([lh, lh, lm, lm, lh, ll], axis=1)
    rhs = jnp.concatenate([rh, rm, rh, rm, rl, rh], axis=0)
    return jnp.dot(lhs, rhs, preferred_element_type=F32)


def symmetric(x):
    return 0.5 * (x + x.T)


GROUP = 4


def left_divide(gram_, right):
    n = gram_.shape[0]
    diag = lax.broadcasted_iota(jnp.int32, (n, n), 0) == lax.broadcasted_iota(jnp.int32, (n, n), 1)
    only = jnp.where(diag, gram_, 0.0)
    down = lax.rsqrt(jnp.sum(only, axis=1, keepdims=True))
    across = lax.rsqrt(jnp.sum(only, axis=0, keepdims=True))
    m = jnp.concatenate([gram_ * across, right], axis=1) * down
    sub = lax.broadcasted_iota(jnp.int32, (n, 1), 0)
    for k in range(0, n, GROUP):
        wide = [jnp.broadcast_to(m[:, k + i:k + i + 1], m.shape) for i in range(GROUP)]
        for i in range(0, GROUP, 2):
            a, b = k + i, k + i + 1
            c0, c1 = wide[i], wide[i + 1]
            p, q, r = c0[a:a + 1, :], c0[b:b + 1, :], c1[b:b + 1, :]
            inverse = 1.0 / (p * r - q * q)

            def eliminate(v):
                r0, r1 = v[a:a + 1, :], v[b:b + 1, :]
                n0 = (r * r0 - q * r1) * inverse
                n1 = (p * r1 - q * r0) * inverse
                return jnp.where(sub == a, n0, jnp.where(sub == b, n1, v - c0 * n0 - c1 * n1))

            for j in range(i + 2, GROUP):
                wide[j] = eliminate(wide[j])
            m = eliminate(m)
    return m[:, n:] * down


FLAT = {"norm": 0, "cross": 32, "sums": 64, "stats": 96}
HALVED = {"norm": (0, 0), "sums": (0, 32), "held_resid": (0, 64), "cross": (1, 0), "held_dir": (1, 32), "held_sol": (1, 64)}


def slot(half):
    return (half + lax.axis_index("ind")) % CORES


def place(ref, name, lanes):
    start = ref.shape[-1] - 128
    if len(ref.shape) == 2:
        start += FLAT[name]
        return slice(0, RHS), slice(start, start + lanes)
    half, lane = HALVED[name]
    start += lane
    return slot(half), slice(0, RHS), slice(start, start + lanes)


def put(ref, name, value):
    ref[place(ref, name, value.shape[1])] = value


def take(ref, name, lanes=RHS):
    return ref[place(ref, name, lanes)]


def put_panel(ref, value):
    width = ref.shape[-1] - 128
    if len(ref.shape) == 2:
        ref[0:RHS, :width] = value
        ref[0:RHS, width:] = jnp.zeros((RHS, 128), F32)
    else:
        for c in range(2):
            ref[slot(c), :, :width] = value[:, c * width:(c + 1) * width]
            ref[slot(c), :, width:] = jnp.zeros((RHS, 128), F32)


def take_panel(ref):
    width = ref.shape[-1] - 128
    if len(ref.shape) == 2:
        return ref[0:RHS, :width]
    return jnp.concatenate([ref[slot(c), :, :width] for c in range(2)], axis=1)


QUARTERS = 4


def prep_kernel(geno_hbm, rhs_hbm, held_hbm, ridge_ref, codes_ref, pay_ref, rhs_ref, lam_ref, chosen_ref,
                geno_ref, held_ref, sems):
    rows, cols = geno_ref.shape
    chunk = rows // QUARTERS
    rhs_copy = pltpu.make_async_copy(rhs_hbm, rhs_ref, sems.at[QUARTERS])
    rhs_copy.start()
    held_copy = pltpu.make_async_copy(held_hbm, held_ref, sems.at[QUARTERS + 1])
    held_copy.start()
    copies = []
    for q in range(QUARTERS):
        part = pl.ds(q * chunk, chunk)
        copies.append(pltpu.make_async_copy(geno_hbm.at[part, :], geno_ref.at[part, :], sems.at[q]))
        copies[-1].start()
    rhs_copy.wait()
    held_copy.wait()
    rhs = rhs_ref[...]
    pieces = stacked(rhs)
    lam_ref[...] = jnp.full(lam_ref.shape, ridge_ref[0], F32)
    norm = gram(pieces, pieces)
    place = lax.broadcasted_iota(jnp.int32, (1, rows), 1) + lax.axis_index("ind") * rows
    chosen_ref[...] = jnp.concatenate([(place == held_ref[:, k:k + 1]).astype(F32) for k in range(RHS)], axis=0).astype(BF16)
    lhs = jnp.concatenate([pieces, jnp.ones((32, rows), BF16)], axis=0)
    panel_, sums, squares = 0.0, 0.0, 0.0
    for q in range(QUARTERS):
        copies[q].wait()
        centred = (geno_ref[q * chunk:(q + 1) * chunk, :] - 1).astype(F32)
        codes = centred.astype(BF16)
        codes_ref[q * chunk:(q + 1) * chunk, :] = codes
        squares = squares + jnp.sum(centred * centred, axis=0, keepdims=True)
        acc = jnp.dot(lhs[:, q * chunk:(q + 1) * chunk], codes, preferred_element_type=F32)
        panel_ = panel_ + fold(acc[:96])
        sums = sums + acc[96:97]
    put_panel(pay_ref, panel_)
    put(pay_ref, "norm", norm)
    put(pay_ref, "sums", jnp.sum(rhs, axis=1, keepdims=True))
    put(pay_ref, "stats", jnp.concatenate([row[:, i:i + 32] for row in (sums, squares) for i in range(0, cols, 32)], axis=0))


def prep(genotypes, rhs, held, ridge):
    rows, cols = genotypes.shape
    hbm = pl.BlockSpec(memory_space=pltpu.HBM)
    return pl.pallas_call(
        prep_kernel,
        in_specs=[hbm, hbm, hbm, pl.BlockSpec(memory_space=pltpu.SMEM)],
        out_shape=[jax.ShapeDtypeStruct((rows, cols), BF16), jax.ShapeDtypeStruct((RHS, cols + 128), F32),
                   jax.ShapeDtypeStruct((RHS, rows), F32), jax.ShapeDtypeStruct((RHS, 128), F32),
                   jax.ShapeDtypeStruct((RHS, rows), BF16)],
        scratch_shapes=[pltpu.VMEM((rows, cols), jnp.int32), pltpu.VMEM(held.shape, jnp.int32),
                        pltpu.SemaphoreType.DMA((QUARTERS + 2,))],
        compiler_params=PARAMS,
        name="prep",
    )(*[pltpu.with_memory_space_constraint(arg, pltpu.HBM) for arg in (genotypes, rhs, held)], ridge)


def panel_kernel(total, first, last, parts, *refs):
    if first:
        red_ref, codes_ref, u_ref, stat_ref, norm_ref, pp_ref, out_ref = refs
    else:
        red_ref, codes_ref, oldu_ref, stat_in_ref, inv_ref, oldpp_ref, u_ref, norm_ref, pp_ref, beta_ref, out_ref = refs
    cols = codes_ref.shape[1]
    if first:
        stats = take(red_ref, "stats")
        sums, squares = [jnp.concatenate([stats[i:i + 1] for i in range(j, j + cols // 32)], axis=1)
                         for j in (0, cols // 32)]
        mean = sums * (1.0 / total)
        scale = 1.0 / jnp.sqrt(squares * (1.0 / total) - mean * mean + 1e-05)
        stat_ref[0:1, :] = mean
        stat_ref[1:2, :] = scale
    else:
        mean, scale = stat_in_ref[0:1, :], stat_in_ref[1:2, :]
    norm = symmetric(take(red_ref, "norm"))
    u = (take_panel(red_ref) - take(red_ref, "sums", 1) * mean) * scale
    norm_ref[...] = norm
    if first:
        pp = norm
    else:
        beta = small_dot(norm, inv_ref[...])
        u = u + small_dot(beta, oldu_ref[...])
        cross = small_dot(beta, take(red_ref, "cross"))
        pp = norm + (cross + cross.T) + symmetric(small_dot(small_dot(beta, oldpp_ref[...]), beta.T))
        beta_ref[...] = beta
    pp_ref[...] = pp
    u_ref[...] = u
    pieces = stacked(u)
    uu = gram(pieces, pieces)
    packed = jnp.concatenate([uu[4 * i:4 * i + 4] for i in range(8)], axis=1)
    if last:
        for j in range(parts):
            out_ref[j, :, :] = packed
        return
    weight = u * scale
    image = fold(lax.dot_general(stacked(weight), codes_ref[...], NT, preferred_element_type=F32))
    image = image - jnp.sum(weight * mean, axis=1, keepdims=True)
    width = image.shape[1] // parts
    for j in range(parts):
        out_ref[j, 0:RHS, :] = image[:, j * width:(j + 1) * width]
        out_ref[j, RHS:, :] = packed


def unpack(block):
    return jnp.concatenate([block[0:4, 32 * i:32 * i + 32] for i in range(8)], axis=0)


def panel(total, first, last, parts, *args):
    rows, cols = args[1].shape
    small = jax.ShapeDtypeStruct((RHS, RHS), F32)
    outs = [jax.ShapeDtypeStruct((RHS, cols), F32)]
    if first:
        outs.append(jax.ShapeDtypeStruct((8, cols), F32))
    outs += [small, small]
    if not first:
        outs.append(small)
    outs.append(jax.ShapeDtypeStruct((parts, 4 if last else RHS + 4, 256), F32))
    return pl.pallas_call(
        functools.partial(panel_kernel, total, first, last, parts),
        out_shape=outs,
        compiler_params=PARAMS,
        name="panel",
    )(*args)


def solve_kernel(markers, first, *refs):
    if first:
        lam_ref, got_ref, pp_ref, norm_ref, resid_ref, send_ref, alpha_ref, inv_ref, sol_ref, base_ref = refs
    else:
        (lam_ref, got_ref, pp_ref, norm_ref, resid_ref, beta_ref, olddir_ref, oldsol_ref,
         send_ref, alpha_ref, inv_ref, sol_ref, base_ref, dir_ref) = refs
    norm = norm_ref[...]
    parts = got_ref.shape[0]
    got = got_ref[0]
    for j in range(1, parts):
        got = got + got_ref[j]
    eye = (lax.broadcasted_iota(jnp.int32, norm.shape, 0) == lax.broadcasted_iota(jnp.int32, norm.shape, 1)).astype(F32)
    curvature = symmetric(unpack(got[RHS:]) * (1.0 / markers) + lam_ref[:, 0:RHS] * pp_ref[...])
    alpha = left_divide(curvature, norm).T
    inv_ref[...] = left_divide(norm, eye)
    alpha_ref[...] = alpha * (1.0 / markers)
    for j in range(parts):
        send_ref[j, :, :] = got[:RHS]
    resid = resid_ref[...]
    if first:
        direction = resid
    else:
        direction = resid + small_dot(beta_ref[...], olddir_ref[...])
        dir_ref[...] = direction
    move = small_dot(alpha, direction)
    sol_ref[...] = move if first else oldsol_ref[...] + move
    base_ref[...] = resid - lam_ref[:, 0:1] * move


def solve(markers, first, *args):
    long = jax.ShapeDtypeStruct(args[4].shape, F32)
    small = jax.ShapeDtypeStruct((RHS, RHS), F32)
    parts, _, width = args[1].shape
    return pl.pallas_call(
        functools.partial(solve_kernel, markers, first),
        out_shape=[jax.ShapeDtypeStruct((parts, RHS, width), F32), small, small, long, long] + ([] if first else [long]),
        compiler_params=PARAMS,
        name="solve",
    )(*args)


def step_kernel(held_too, *refs):
    if held_too:
        image_ref, alpha_ref, base_ref, dir_ref, codes_ref, sol_ref, chosen_ref, resid_ref, pay_ref = refs
    else:
        image_ref, alpha_ref, base_ref, dir_ref, codes_ref, resid_ref, pay_ref = refs
    image = jnp.concatenate([image_ref[j] for j in range(image_ref.shape[0])], axis=1)
    resid = base_ref[...] - small_dot(alpha_ref[...], image)
    resid_ref[...] = resid
    pieces = stacked(resid)
    dpieces = stacked(dir_ref[...])
    put_panel(pay_ref, fold(jnp.dot(pieces, codes_ref[...], preferred_element_type=F32)))
    put(pay_ref, "norm", gram(pieces, pieces))
    put(pay_ref, "sums", jnp.sum(resid, axis=1, keepdims=True))
    put(pay_ref, "cross", gram(dpieces, pieces))
    if held_too:
        chosen = chosen_ref[...]
        for name, value in (("held_resid", pieces), ("held_dir", dpieces), ("held_sol", stacked(sol_ref[...]))):
            put(pay_ref, name, fold(lax.dot_general(value, chosen, NT, preferred_element_type=F32)))


def step(held_too, *args):
    rows, cols = args[4].shape
    return pl.pallas_call(
        functools.partial(step_kernel, held_too),
        out_shape=[jax.ShapeDtypeStruct((RHS, rows), F32),
                   jax.ShapeDtypeStruct((2, RHS, cols // 2 + 128) if held_too else (RHS, cols + 128), F32)],
        compiler_params=PARAMS,
        name="step",
    )(*args)


def last_kernel(markers, lam_ref, got_ref, pp_ref, norm_ref, beta_ref, resid_ref, olddir_ref, sol_ref, red_ref,
                out_ref, held_ref):
    got = got_ref[0]
    for j in range(1, got_ref.shape[0]):
        got = got + got_ref[j]
    alpha = left_divide(symmetric(unpack(got) * (1.0 / markers) + lam_ref[:, 0:RHS] * pp_ref[...]), norm_ref[...]).T
    beta = beta_ref[...]
    out_ref[...] = sol_ref[...] + small_dot(alpha, resid_ref[...] + small_dot(beta, olddir_ref[...]))
    direction = take(red_ref, "held_resid") + small_dot(beta, take(red_ref, "held_dir"))
    rows = take(red_ref, "held_sol") + small_dot(alpha, direction)
    eye = lax.broadcasted_iota(jnp.int32, rows.shape, 0) == lax.broadcasted_iota(jnp.int32, rows.shape, 1)
    held_ref[...] = jnp.sum(jnp.where(eye, rows, 0.0), axis=0, keepdims=True)


def last_step(markers, *args):
    return pl.pallas_call(
        functools.partial(last_kernel, markers),
        out_shape=[jax.ShapeDtypeStruct(args[5].shape, F32), jax.ShapeDtypeStruct((1, RHS), F32)],
        compiler_params=PARAMS,
        name="last",
    )(*args)


def on_ind(move):
    pairs = []
    for y in range(YSIZE):
        for x in range(XSIZE):
            for c in range(CORES):
                ty, tx, tc = move(y, x, c)
                pairs.append(((y * XSIZE + x) * CORES + c, (ty * XSIZE + tx) * CORES + tc))
    return pairs


def swap_cores(value):
    return lax.ppermute(value, "ind", on_ind(lambda y, x, c: (y, x, 1 - c)))


def sum_chips(value):
    for along in ("x", "y"):
        moved = {}
        for d in (1, 3, 2):
            if along == "x":
                pairs = on_ind(lambda y, x, c, d=d: (y, (x + d) % XSIZE, c))
            else:
                pairs = on_ind(lambda y, x, c, d=d: ((y + d) % YSIZE, x, c))
            moved[d] = lax.ppermute(value, "ind", pairs)
        value = (moved[3] + moved[1]) + (moved[2] + value)
    return value


def sum_ind(value):
    if value.ndim == 2:
        return sum_chips(value + swap_cores(value))
    mine = sum_chips(value[0] + swap_cores(value[1]))
    return jnp.stack([mine, swap_cores(mine)])


def exchange(value):
    return lax.all_to_all(value, "snp", 0, 0)


def shards(genotypes, targets, ridge, held_out):
    rows, cols = genotypes.shape
    parts = lax.axis_size("snp")
    total = rows * lax.axis_size("ind")
    markers = cols * parts

    codes, pay, resid, lam, chosen = prep(genotypes, targets.T, held_out[None, :], ridge)
    for k in range(ITERS):
        first, last = k == 0, k == ITERS - 1
        red = sum_ind(pay)
        if first:
            u, stat, norm, pp, out = panel(total, True, False, parts, red, codes)
        else:
            u, norm, pp, beta, out = panel(total, False, last, parts, red, codes, u, stat, inv, pp)
        got = exchange(out)
        if last:
            break
        args = [lam, got, pp, norm, resid]
        if first:
            direction = resid
            send, alpha, inv, sol, base = solve(markers, True, *args)
        else:
            send, alpha, inv, sol, base, direction = solve(markers, False, *args, beta, direction, sol)
        image = exchange(send)
        held_too = k == ITERS - 2
        resid, pay = step(held_too, image, alpha, base, direction, codes, *([sol, chosen] if held_too else []))
    sol, held = last_step(markers, lam, got, pp, norm, beta, resid, direction, sol, red)
    return sol.T, held[0]


def solution(mesh):
    return jax.shard_map(
        shards,
        mesh=mesh,
        in_specs=(P("ind", "snp"), P("ind", None), P(), P()),
        out_specs=(P("ind", None), P()),
        check_vma=False,
    )
```

```python
import functools

import jax
import jax.numpy as jnp
from jax import lax
from jax.experimental import pallas as pl
from jax.experimental.pallas import tpu as pltpu
from jax.sharding import PartitionSpec as P

ITERS = 4
RHS = 32
XSIZE, YSIZE, CORES = 4, 4, 2
F32, BF16 = jnp.float32, jnp.bfloat16
NT = (((1,), (1,)), ((), ()))
PARAMS = pltpu.CompilerParams(vmem_limit_bytes=12 * 1024 * 1024)


def split(x):
    high = x.astype(BF16)
    rest = x - high.astype(F32)
    mid = rest.astype(BF16)
    low = (rest - mid.astype(F32)).astype(BF16)
    return high, mid, low


def stacked(x):
    return jnp.concatenate(split(x), axis=0)


def fold(x):
    n = x.shape[0] // 3
    return x[:n] + (x[n:2 * n] + x[2 * n:])


def gram(left, right):
    full = fold(lax.dot_general(left, right, NT, preferred_element_type=F32))
    n = full.shape[1] // 3
    return full[:, :n] + (full[:, n:2 * n] + full[:, 2 * n:])


def small_dot(left, right):
    lh, lm, ll = split(left)
    rh, rm, rl = split(right)
    lhs = jnp.concatenate([lh, lh, lm, lm, lh, ll], axis=1)
    rhs = jnp.concatenate([rh, rm, rh, rm, rl, rh], axis=0)
    return jnp.dot(lhs, rhs, preferred_element_type=F32)


def symmetric(x):
    return 0.5 * (x + x.T)


GROUP = 4


def left_divide(gram_, right):
    n = gram_.shape[0]
    diag = lax.broadcasted_iota(jnp.int32, (n, n), 0) == lax.broadcasted_iota(jnp.int32, (n, n), 1)
    only = jnp.where(diag, gram_, 0.0)
    down = lax.rsqrt(jnp.sum(only, axis=1, keepdims=True))
    across = lax.rsqrt(jnp.sum(only, axis=0, keepdims=True))
    m = jnp.concatenate([gram_ * across, right], axis=1) * down
    sub = lax.broadcasted_iota(jnp.int32, (n, 1), 0)
    for k in range(0, n, GROUP):
        wide = [jnp.broadcast_to(m[:, k + i:k + i + 1], m.shape) for i in range(GROUP)]
        for i in range(0, GROUP, 2):
            a, b = k + i, k + i + 1
            c0, c1 = wide[i], wide[i + 1]
            p, q, r = c0[a:a + 1, :], c0[b:b + 1, :], c1[b:b + 1, :]
            inverse = 1.0 / (p * r - q * q)

            def eliminate(v):
                r0, r1 = v[a:a + 1, :], v[b:b + 1, :]
                n0 = (r * r0 - q * r1) * inverse
                n1 = (p * r1 - q * r0) * inverse
                return jnp.where(sub == a, n0, jnp.where(sub == b, n1, v - c0 * n0 - c1 * n1))

            for j in range(i + 2, GROUP):
                wide[j] = eliminate(wide[j])
            m = eliminate(m)
    return m[:, n:] * down


SIDE = {"norm": 0, "held": 32, "sums": 64, "cross": 96, "stats": 96}


def put(ref, name, value):
    lane = ref.shape[1] - 128 + SIDE[name]
    ref[:, lane:lane + value.shape[1]] = value


def take(ref, name, lanes=RHS):
    lane = ref.shape[1] - 128 + SIDE[name]
    return ref[:, lane:lane + lanes]


def put_panel(ref, value):
    cols = value.shape[1]
    ref[:, :cols] = value
    ref[:, cols:] = jnp.zeros((RHS, ref.shape[1] - cols), F32)


def rows_at(pieces, chosen):
    return fold(lax.dot_general(pieces, chosen, NT, preferred_element_type=F32))


QUARTERS = 4


def prep_kernel(geno_hbm, rhs_hbm, held_hbm, ridge_ref, codes_ref, pay_ref, rhs_ref, lam_ref, chosen_ref,
                geno_ref, held_ref, sems):
    rows, cols = geno_ref.shape
    chunk = rows // QUARTERS
    rhs_copy = pltpu.make_async_copy(rhs_hbm, rhs_ref, sems.at[QUARTERS])
    rhs_copy.start()
    held_copy = pltpu.make_async_copy(held_hbm, held_ref, sems.at[QUARTERS + 1])
    held_copy.start()
    copies = []
    for q in range(QUARTERS):
        part = pl.ds(q * chunk, chunk)
        copies.append(pltpu.make_async_copy(geno_hbm.at[part, :], geno_ref.at[part, :], sems.at[q]))
        copies[-1].start()
    rhs_copy.wait()
    held_copy.wait()
    rhs = rhs_ref[...]
    pieces = stacked(rhs)
    lam_ref[...] = jnp.full(lam_ref.shape, ridge_ref[0], F32)
    norm = gram(pieces, pieces)
    place = lax.broadcasted_iota(jnp.int32, (1, rows), 1) + lax.axis_index("ind") * rows
    chosen_ref[...] = jnp.concatenate([(place == held_ref[:, k:k + 1]).astype(F32) for k in range(RHS)], axis=0).astype(BF16)
    lhs = jnp.concatenate([pieces, jnp.ones((32, rows), BF16)], axis=0)
    panel_, sums, squares = 0.0, 0.0, 0.0
    for q in range(QUARTERS):
        copies[q].wait()
        centred = (geno_ref[q * chunk:(q + 1) * chunk, :] - 1).astype(F32)
        codes = centred.astype(BF16)
        codes_ref[q * chunk:(q + 1) * chunk, :] = codes
        squares = squares + jnp.sum(centred * centred, axis=0, keepdims=True)
        acc = jnp.dot(lhs[:, q * chunk:(q + 1) * chunk], codes, preferred_element_type=F32)
        panel_ = panel_ + fold(acc[:96])
        sums = sums + acc[96:97]
    put_panel(pay_ref, panel_)
    put(pay_ref, "norm", norm)
    put(pay_ref, "sums", jnp.sum(rhs, axis=1, keepdims=True))
    put(pay_ref, "held", rows_at(pieces, chosen_ref[...]))
    put(pay_ref, "stats", jnp.concatenate([row[:, i:i + 32] for row in (sums, squares) for i in range(0, cols, 32)], axis=0))


def prep(genotypes, rhs, held, ridge):
    rows, cols = genotypes.shape
    hbm = pl.BlockSpec(memory_space=pltpu.HBM)
    return pl.pallas_call(
        prep_kernel,
        in_specs=[hbm, hbm, hbm, pl.BlockSpec(memory_space=pltpu.SMEM)],
        out_shape=[jax.ShapeDtypeStruct((rows, cols), BF16), jax.ShapeDtypeStruct((RHS, cols + 128), F32),
                   jax.ShapeDtypeStruct((RHS, rows), F32), jax.ShapeDtypeStruct((RHS, 128), F32),
                   jax.ShapeDtypeStruct((RHS, rows), BF16)],
        scratch_shapes=[pltpu.VMEM((rows, cols), jnp.int32), pltpu.VMEM(held.shape, jnp.int32),
                        pltpu.SemaphoreType.DMA((QUARTERS + 2,))],
        compiler_params=PARAMS,
        name="prep",
    )(*[pltpu.with_memory_space_constraint(arg, pltpu.HBM) for arg in (genotypes, rhs, held)], ridge)


def panel_kernel(total, first, last, parts, *refs):
    if first:
        red_ref, codes_ref, u_ref, stat_ref, norm_ref, pp_ref, heldp_ref, out_ref = refs
    else:
        red_ref, codes_ref, oldu_ref, stat_in_ref, inv_ref, oldpp_ref, oldheldp_ref = refs[:7]
        norm_ref, pp_ref, heldp_ref, beta_ref, out_ref = refs[-5:]
        u_ref = None if last else refs[7]
    cols = codes_ref.shape[1]
    if first:
        stats = take(red_ref, "stats")
        sums, squares = [jnp.concatenate([stats[i:i + 1] for i in range(j, j + cols // 32)], axis=1)
                         for j in (0, cols // 32)]
        mean = sums * (1.0 / total)
        scale = 1.0 / jnp.sqrt(squares * (1.0 / total) - mean * mean + 1e-05)
        stat_ref[0:1, :] = mean
        stat_ref[1:2, :] = scale
    else:
        mean, scale = stat_in_ref[0:1, :], stat_in_ref[1:2, :]
    norm = symmetric(take(red_ref, "norm"))
    u = (red_ref[:, :cols] - take(red_ref, "sums", 1) * mean) * scale
    norm_ref[...] = norm
    held = take(red_ref, "held")
    if first:
        pp = norm
        heldp_ref[...] = held
    else:
        beta = small_dot(norm, inv_ref[...])
        u = u + small_dot(beta, oldu_ref[...])
        cross = small_dot(beta, take(red_ref, "cross"))
        pp = norm + (cross + cross.T) + symmetric(small_dot(small_dot(beta, oldpp_ref[...]), beta.T))
        heldp_ref[...] = held + small_dot(beta, oldheldp_ref[...])
        beta_ref[...] = beta
    pp_ref[...] = pp
    if not last:
        u_ref[...] = u
    pieces = stacked(u)
    uu = gram(pieces, pieces)
    packed = jnp.concatenate([uu[4 * i:4 * i + 4] for i in range(8)], axis=1)
    if last:
        for j in range(parts):
            out_ref[j, :, :] = packed
        return
    weight = u * scale
    image = fold(lax.dot_general(stacked(weight), codes_ref[...], NT, preferred_element_type=F32))
    image = image - jnp.sum(weight * mean, axis=1, keepdims=True)
    width = image.shape[1] // parts
    for j in range(parts):
        out_ref[j, 0:RHS, :] = image[:, j * width:(j + 1) * width]
        out_ref[j, RHS:, :] = packed


def unpack(block):
    return jnp.concatenate([block[0:4, 32 * i:32 * i + 32] for i in range(8)], axis=0)


def panel(total, first, last, parts, *args):
    rows, cols = args[1].shape
    small = jax.ShapeDtypeStruct((RHS, RHS), F32)
    outs = [] if last else [jax.ShapeDtypeStruct((RHS, cols), F32)]
    if first:
        outs.append(jax.ShapeDtypeStruct((8, cols), F32))
    outs += [small, small, small]
    if not first:
        outs.append(small)
    outs.append(jax.ShapeDtypeStruct((parts, 4 if last else RHS + 4, 256), F32))
    return pl.pallas_call(
        functools.partial(panel_kernel, total, first, last, parts),
        out_shape=outs,
        compiler_params=PARAMS,
        name="panel",
    )(*args)


def solve_kernel(markers, first, *refs):
    if first:
        (lam_ref, got_ref, pp_ref, norm_ref, resid_ref, heldp_ref,
         send_ref, alpha_ref, inv_ref, heldx_ref, sol_ref, base_ref) = refs
    else:
        (lam_ref, got_ref, pp_ref, norm_ref, resid_ref, heldp_ref, oldheldx_ref, beta_ref, olddir_ref, oldsol_ref,
         send_ref, alpha_ref, inv_ref, heldx_ref, sol_ref, base_ref, dir_ref) = refs
    norm = norm_ref[...]
    parts = got_ref.shape[0]
    got = got_ref[0]
    for j in range(1, parts):
        got = got + got_ref[j]
    eye = (lax.broadcasted_iota(jnp.int32, norm.shape, 0) == lax.broadcasted_iota(jnp.int32, norm.shape, 1)).astype(F32)
    curvature = symmetric(unpack(got[RHS:]) * (1.0 / markers) + lam_ref[:, 0:RHS] * pp_ref[...])
    alpha = left_divide(curvature, norm).T
    inv_ref[...] = left_divide(norm, eye)
    alpha_ref[...] = alpha * (1.0 / markers)
    for j in range(parts):
        send_ref[j, :, :] = got[:RHS]
    resid = resid_ref[...]
    if first:
        direction = resid
    else:
        direction = resid + small_dot(beta_ref[...], olddir_ref[...])
        dir_ref[...] = direction
    heldx = small_dot(alpha, heldp_ref[...])
    heldx_ref[...] = heldx if first else oldheldx_ref[...] + heldx
    move = small_dot(alpha, direction)
    sol_ref[...] = move if first else oldsol_ref[...] + move
    base_ref[...] = resid - lam_ref[:, 0:1] * move


def solve(markers, first, *args):
    long = jax.ShapeDtypeStruct(args[4].shape, F32)
    small = jax.ShapeDtypeStruct((RHS, RHS), F32)
    parts, _, width = args[1].shape
    return pl.pallas_call(
        functools.partial(solve_kernel, markers, first),
        out_shape=[jax.ShapeDtypeStruct((parts, RHS, width), F32), small, small, small, long, long] + ([] if first else [long]),
        compiler_params=PARAMS,
        name="solve",
    )(*args)


def step_kernel(image_ref, alpha_ref, base_ref, dir_ref, codes_ref, chosen_ref, resid_ref, pay_ref):
    image = jnp.concatenate([image_ref[j] for j in range(image_ref.shape[0])], axis=1)
    resid = base_ref[...] - small_dot(alpha_ref[...], image)
    resid_ref[...] = resid
    pieces = stacked(resid)
    dpieces = stacked(dir_ref[...])
    put_panel(pay_ref, fold(jnp.dot(pieces, codes_ref[...], preferred_element_type=F32)))
    put(pay_ref, "norm", gram(pieces, pieces))
    put(pay_ref, "sums", jnp.sum(resid, axis=1, keepdims=True))
    put(pay_ref, "cross", gram(dpieces, pieces))
    put(pay_ref, "held", rows_at(pieces, chosen_ref[...]))


def step(*args):
    rows, cols = args[4].shape
    return pl.pallas_call(
        step_kernel,
        out_shape=[jax.ShapeDtypeStruct((RHS, rows), F32), jax.ShapeDtypeStruct((RHS, cols + 128), F32)],
        compiler_params=PARAMS,
        name="step",
    )(*args)


def last_kernel(markers, lam_ref, got_ref, pp_ref, norm_ref, beta_ref, resid_ref, olddir_ref, sol_ref, heldp_ref,
                heldx_ref, out_ref, held_ref):
    got = got_ref[0]
    for j in range(1, got_ref.shape[0]):
        got = got + got_ref[j]
    alpha = left_divide(symmetric(unpack(got) * (1.0 / markers) + lam_ref[:, 0:RHS] * pp_ref[...]), norm_ref[...]).T
    beta = beta_ref[...]
    out_ref[...] = sol_ref[...] + small_dot(alpha, resid_ref[...] + small_dot(beta, olddir_ref[...]))
    rows = heldx_ref[...] + small_dot(alpha, heldp_ref[...])
    eye = lax.broadcasted_iota(jnp.int32, rows.shape, 0) == lax.broadcasted_iota(jnp.int32, rows.shape, 1)
    held_ref[...] = jnp.sum(jnp.where(eye, rows, 0.0), axis=0, keepdims=True)


def last_step(markers, *args):
    return pl.pallas_call(
        functools.partial(last_kernel, markers),
        out_shape=[jax.ShapeDtypeStruct(args[5].shape, F32), jax.ShapeDtypeStruct((1, RHS), F32)],
        compiler_params=PARAMS,
        name="last",
    )(*args)


def on_ind(move):
    pairs = []
    for y in range(YSIZE):
        for x in range(XSIZE):
            for c in range(CORES):
                ty, tx, tc = move(y, x, c)
                pairs.append(((y * XSIZE + x) * CORES + c, (ty * XSIZE + tx) * CORES + tc))
    return pairs


def swap_cores(value):
    return lax.ppermute(value, "ind", on_ind(lambda y, x, c: (y, x, 1 - c)))


def sum_ind(value):
    value = value + swap_cores(value)
    for along in ("x", "y"):
        moved = {}
        for d in (1, 3, 2):
            if along == "x":
                pairs = on_ind(lambda y, x, c, d=d: (y, (x + d) % XSIZE, c))
            else:
                pairs = on_ind(lambda y, x, c, d=d: ((y + d) % YSIZE, x, c))
            moved[d] = lax.ppermute(value, "ind", pairs)
        value = (moved[3] + moved[1]) + (moved[2] + value)
    return value


def exchange(value):
    return lax.all_to_all(value, "snp", 0, 0)


def shards(genotypes, targets, ridge, held_out):
    rows, cols = genotypes.shape
    parts = lax.axis_size("snp")
    total = rows * lax.axis_size("ind")
    markers = cols * parts

    codes, pay, resid, lam, chosen = prep(genotypes, targets.T, held_out[None, :], ridge)
    for k in range(ITERS):
        first, last = k == 0, k == ITERS - 1
        red = sum_ind(pay)
        if first:
            u, stat, norm, pp, heldp, out = panel(total, True, False, parts, red, codes)
        else:
            *new_u, norm, pp, heldp, beta, out = panel(total, False, last, parts, red, codes, u, stat, inv, pp, heldp)
            u = new_u[0] if new_u else None
        got = exchange(out)
        if last:
            break
        args = [lam, got, pp, norm, resid, heldp]
        if first:
            direction = resid
            send, alpha, inv, heldx, sol, base = solve(markers, True, *args)
        else:
            send, alpha, inv, heldx, sol, base, direction = solve(
                markers, False, *args, heldx, beta, direction, sol)
        image = exchange(send)
        resid, pay = step(image, alpha, base, direction, codes, chosen)
    sol, held = last_step(markers, lam, got, pp, norm, beta, resid, direction, sol, heldp, heldx)
    return sol.T, held[0]


def solution(mesh):
    return jax.shard_map(
        shards,
        mesh=mesh,
        in_specs=(P("ind", "snp"), P("ind", None), P(), P()),
        out_specs=(P("ind", None), P()),
        check_vma=False,
    )
```

```python
import functools

import jax
import jax.numpy as jnp
from jax import lax
from jax.experimental import pallas as pl
from jax.experimental.pallas import tpu as pltpu
from jax.sharding import PartitionSpec as P

ITERS = 4
RHS = 32
XSIZE, YSIZE, CORES = 4, 4, 2
F32, BF16 = jnp.float32, jnp.bfloat16
NT = (((1,), (1,)), ((), ()))
PARAMS = pltpu.CompilerParams(vmem_limit_bytes=12 * 1024 * 1024)


def split(x):
    high = x.astype(BF16)
    rest = x - high.astype(F32)
    mid = rest.astype(BF16)
    low = (rest - mid.astype(F32)).astype(BF16)
    return high, mid, low


def stacked(x):
    return jnp.concatenate(split(x), axis=0)


def fold(x):
    n = x.shape[0] // 3
    return x[:n] + (x[n:2 * n] + x[2 * n:])


def gram(left, right):
    full = fold(lax.dot_general(left, right, NT, preferred_element_type=F32))
    n = full.shape[1] // 3
    return full[:, :n] + (full[:, n:2 * n] + full[:, 2 * n:])


def small_dot(left, right):
    lh, lm, ll = split(left)
    rh, rm, rl = split(right)
    lhs = jnp.concatenate([lh, lh, lm, lm, lh, ll], axis=1)
    rhs = jnp.concatenate([rh, rm, rh, rm, rl, rh], axis=0)
    return jnp.dot(lhs, rhs, preferred_element_type=F32)


def symmetric(x):
    return 0.5 * (x + x.T)


GROUP = 4


def left_divide(gram_, right):
    n = gram_.shape[0]
    diag = lax.broadcasted_iota(jnp.int32, (n, n), 0) == lax.broadcasted_iota(jnp.int32, (n, n), 1)
    only = jnp.where(diag, gram_, 0.0)
    down = lax.rsqrt(jnp.sum(only, axis=1, keepdims=True))
    across = lax.rsqrt(jnp.sum(only, axis=0, keepdims=True))
    m = jnp.concatenate([gram_ * across, right], axis=1) * down
    sub = lax.broadcasted_iota(jnp.int32, (n, 1), 0)
    for k in range(0, n, GROUP):
        wide = [jnp.broadcast_to(m[:, k + i:k + i + 1], m.shape) for i in range(GROUP)]
        for i in range(0, GROUP, 2):
            a, b = k + i, k + i + 1
            c0, c1 = wide[i], wide[i + 1]
            p, q, r = c0[a:a + 1, :], c0[b:b + 1, :], c1[b:b + 1, :]
            inverse = 1.0 / (p * r - q * q)

            def eliminate(v):
                r0, r1 = v[a:a + 1, :], v[b:b + 1, :]
                n0 = (r * r0 - q * r1) * inverse
                n1 = (p * r1 - q * r0) * inverse
                return jnp.where(sub == a, n0, jnp.where(sub == b, n1, v - c0 * n0 - c1 * n1))

            for j in range(i + 2, GROUP):
                wide[j] = eliminate(wide[j])
            m = eliminate(m)
    return m[:, n:] * down


SIDE = {"norm": 0, "held": 32, "sums": 64, "cross": 96, "stats": 96}


def put(ref, name, value):
    lane = ref.shape[1] - 128 + SIDE[name]
    ref[:, lane:lane + value.shape[1]] = value


def take(ref, name, lanes=RHS):
    lane = ref.shape[1] - 128 + SIDE[name]
    return ref[:, lane:lane + lanes]


def put_panel(ref, value):
    cols = value.shape[1]
    ref[:, :cols] = value
    ref[:, cols:] = jnp.zeros((RHS, ref.shape[1] - cols), F32)


def rows_at(pieces, chosen):
    return fold(lax.dot_general(pieces, chosen, NT, preferred_element_type=F32))


CHUNKS = 8


def prep_kernel(geno_hbm, rhs_hbm, held_hbm, ridge_ref, codes_ref, pay_ref, rhs_ref, lam_ref, chosen_ref,
                geno_ref, held_ref, sems):
    rows, cols = geno_ref.shape
    chunk = rows // CHUNKS
    rhs_copy = pltpu.make_async_copy(rhs_hbm, rhs_ref, sems.at[CHUNKS])
    rhs_copy.start()
    held_copy = pltpu.make_async_copy(held_hbm, held_ref, sems.at[CHUNKS + 1])
    held_copy.start()
    copies = []
    for q in range(CHUNKS):
        part = pl.ds(q * chunk, chunk)
        copies.append(pltpu.make_async_copy(geno_hbm.at[part, :], geno_ref.at[part, :], sems.at[q]))
        copies[-1].start()
    rhs_copy.wait()
    held_copy.wait()
    rhs = rhs_ref[...]
    pieces = stacked(rhs)
    lam_ref[...] = jnp.full(lam_ref.shape, ridge_ref[0], F32)
    norm = gram(pieces, pieces)
    place = lax.broadcasted_iota(jnp.int32, (1, rows), 1) + lax.axis_index("ind") * rows
    chosen_ref[...] = jnp.concatenate([(place == held_ref[:, k:k + 1]).astype(F32) for k in range(RHS)], axis=0).astype(BF16)
    lhs = jnp.concatenate([pieces, jnp.ones((32, rows), BF16)], axis=0)
    panel_, sums, squares = 0.0, 0.0, 0.0
    for q in range(CHUNKS):
        copies[q].wait()
        centred = (geno_ref[q * chunk:(q + 1) * chunk, :] - 1).astype(F32)
        codes = centred.astype(BF16)
        codes_ref[q * chunk:(q + 1) * chunk, :] = codes
        squares = squares + jnp.sum(centred * centred, axis=0, keepdims=True)
        acc = jnp.dot(lhs[:, q * chunk:(q + 1) * chunk], codes, preferred_element_type=F32)
        panel_ = panel_ + fold(acc[:96])
        sums = sums + acc[96:97]
    put_panel(pay_ref, panel_)
    put(pay_ref, "norm", norm)
    put(pay_ref, "sums", jnp.sum(rhs, axis=1, keepdims=True))
    put(pay_ref, "held", rows_at(pieces, chosen_ref[...]))
    put(pay_ref, "stats", jnp.concatenate([row[:, i:i + 32] for row in (sums, squares) for i in range(0, cols, 32)], axis=0))


def prep(genotypes, rhs, held, ridge):
    rows, cols = genotypes.shape
    hbm = pl.BlockSpec(memory_space=pltpu.HBM)
    return pl.pallas_call(
        prep_kernel,
        in_specs=[hbm, hbm, hbm, pl.BlockSpec(memory_space=pltpu.SMEM)],
        out_shape=[jax.ShapeDtypeStruct((rows, cols), BF16), jax.ShapeDtypeStruct((RHS, cols + 128), F32),
                   jax.ShapeDtypeStruct((RHS, rows), F32), jax.ShapeDtypeStruct((RHS, 128), F32),
                   jax.ShapeDtypeStruct((RHS, rows), BF16)],
        scratch_shapes=[pltpu.VMEM((rows, cols), jnp.int32), pltpu.VMEM(held.shape, jnp.int32),
                        pltpu.SemaphoreType.DMA((CHUNKS + 2,))],
        compiler_params=PARAMS,
        name="prep",
    )(*[pltpu.with_memory_space_constraint(arg, pltpu.HBM) for arg in (genotypes, rhs, held)], ridge)


def panel_kernel(total, first, last, parts, *refs):
    if first:
        red_ref, codes_ref, u_ref, stat_ref, norm_ref, pp_ref, heldp_ref, out_ref = refs
    else:
        red_ref, codes_ref, oldu_ref, stat_in_ref, inv_ref, oldpp_ref, oldheldp_ref = refs[:7]
        norm_ref, pp_ref, heldp_ref, beta_ref, out_ref = refs[-5:]
        u_ref = None if last else refs[7]
    cols = codes_ref.shape[1]
    if first:
        stats = take(red_ref, "stats")
        sums, squares = [jnp.concatenate([stats[i:i + 1] for i in range(j, j + cols // 32)], axis=1)
                         for j in (0, cols // 32)]
        mean = sums * (1.0 / total)
        scale = 1.0 / jnp.sqrt(squares * (1.0 / total) - mean * mean + 1e-05)
        stat_ref[0:1, :] = mean
        stat_ref[1:2, :] = scale
    else:
        mean, scale = stat_in_ref[0:1, :], stat_in_ref[1:2, :]
    norm = symmetric(take(red_ref, "norm"))
    u = (red_ref[:, :cols] - take(red_ref, "sums", 1) * mean) * scale
    norm_ref[...] = norm
    held = take(red_ref, "held")
    if first:
        pp = norm
        heldp_ref[...] = held
    else:
        beta = small_dot(norm, inv_ref[...])
        u = u + small_dot(beta, oldu_ref[...])
        cross = small_dot(beta, take(red_ref, "cross"))
        pp = norm + (cross + cross.T) + symmetric(small_dot(small_dot(beta, oldpp_ref[...]), beta.T))
        heldp_ref[...] = held + small_dot(beta, oldheldp_ref[...])
        beta_ref[...] = beta
    pp_ref[...] = pp
    if not last:
        u_ref[...] = u
    pieces = stacked(u)
    uu = gram(pieces, pieces)
    packed = jnp.concatenate([uu[4 * i:4 * i + 4] for i in range(8)], axis=1)
    if last:
        for j in range(parts):
            out_ref[j, :, :] = packed
        return
    weight = u * scale
    image = fold(lax.dot_general(stacked(weight), codes_ref[...], NT, preferred_element_type=F32))
    image = image - jnp.sum(weight * mean, axis=1, keepdims=True)
    width = image.shape[1] // parts
    for j in range(parts):
        out_ref[j, 0:RHS, :] = image[:, j * width:(j + 1) * width]
        out_ref[j, RHS:, :] = packed


def unpack(block):
    return jnp.concatenate([block[0:4, 32 * i:32 * i + 32] for i in range(8)], axis=0)


def panel(total, first, last, parts, *args):
    rows, cols = args[1].shape
    small = jax.ShapeDtypeStruct((RHS, RHS), F32)
    outs = [] if last else [jax.ShapeDtypeStruct((RHS, cols), F32)]
    if first:
        outs.append(jax.ShapeDtypeStruct((8, cols), F32))
    outs += [small, small, small]
    if not first:
        outs.append(small)
    outs.append(jax.ShapeDtypeStruct((parts, 4 if last else RHS + 4, 256), F32))
    return pl.pallas_call(
        functools.partial(panel_kernel, total, first, last, parts),
        out_shape=outs,
        compiler_params=PARAMS,
        name="panel",
    )(*args)


def solve_kernel(markers, first, *refs):
    if first:
        (lam_ref, got_ref, pp_ref, norm_ref, resid_ref, heldp_ref,
         send_ref, alpha_ref, inv_ref, heldx_ref, sol_ref, base_ref) = refs
    else:
        (lam_ref, got_ref, pp_ref, norm_ref, resid_ref, heldp_ref, oldheldx_ref, beta_ref, olddir_ref, oldsol_ref,
         send_ref, alpha_ref, inv_ref, heldx_ref, sol_ref, base_ref, dir_ref) = refs
    norm = norm_ref[...]
    parts = got_ref.shape[0]
    got = got_ref[0]
    for j in range(1, parts):
        got = got + got_ref[j]
    eye = (lax.broadcasted_iota(jnp.int32, norm.shape, 0) == lax.broadcasted_iota(jnp.int32, norm.shape, 1)).astype(F32)
    curvature = symmetric(unpack(got[RHS:]) * (1.0 / markers) + lam_ref[:, 0:RHS] * pp_ref[...])
    alpha = left_divide(curvature, norm).T
    inv_ref[...] = left_divide(norm, eye)
    alpha_ref[...] = alpha * (1.0 / markers)
    for j in range(parts):
        send_ref[j, :, :] = got[:RHS]
    resid = resid_ref[...]
    if first:
        direction = resid
    else:
        direction = resid + small_dot(beta_ref[...], olddir_ref[...])
        dir_ref[...] = direction
    heldx = small_dot(alpha, heldp_ref[...])
    heldx_ref[...] = heldx if first else oldheldx_ref[...] + heldx
    move = small_dot(alpha, direction)
    sol_ref[...] = move if first else oldsol_ref[...] + move
    base_ref[...] = resid - lam_ref[:, 0:1] * move


def solve(markers, first, *args):
    long = jax.ShapeDtypeStruct(args[4].shape, F32)
    small = jax.ShapeDtypeStruct((RHS, RHS), F32)
    parts, _, width = args[1].shape
    return pl.pallas_call(
        functools.partial(solve_kernel, markers, first),
        out_shape=[jax.ShapeDtypeStruct((parts, RHS, width), F32), small, small, small, long, long] + ([] if first else [long]),
        compiler_params=PARAMS,
        name="solve",
    )(*args)


def step_kernel(image_ref, alpha_ref, base_ref, dir_ref, codes_ref, chosen_ref, resid_ref, pay_ref):
    image = jnp.concatenate([image_ref[j] for j in range(image_ref.shape[0])], axis=1)
    resid = base_ref[...] - small_dot(alpha_ref[...], image)
    resid_ref[...] = resid
    pieces = stacked(resid)
    dpieces = stacked(dir_ref[...])
    put_panel(pay_ref, fold(jnp.dot(pieces, codes_ref[...], preferred_element_type=F32)))
    put(pay_ref, "norm", gram(pieces, pieces))
    put(pay_ref, "sums", jnp.sum(resid, axis=1, keepdims=True))
    put(pay_ref, "cross", gram(dpieces, pieces))
    put(pay_ref, "held", rows_at(pieces, chosen_ref[...]))


def step(*args):
    rows, cols = args[4].shape
    return pl.pallas_call(
        step_kernel,
        out_shape=[jax.ShapeDtypeStruct((RHS, rows), F32), jax.ShapeDtypeStruct((RHS, cols + 128), F32)],
        compiler_params=PARAMS,
        name="step",
    )(*args)


def last_kernel(markers, lam_ref, got_ref, pp_ref, norm_ref, beta_ref, resid_ref, olddir_ref, sol_ref, heldp_ref,
                heldx_ref, out_ref, held_ref):
    got = got_ref[0]
    for j in range(1, got_ref.shape[0]):
        got = got + got_ref[j]
    alpha = left_divide(symmetric(unpack(got) * (1.0 / markers) + lam_ref[:, 0:RHS] * pp_ref[...]), norm_ref[...]).T
    beta = beta_ref[...]
    out_ref[...] = sol_ref[...] + small_dot(alpha, resid_ref[...] + small_dot(beta, olddir_ref[...]))
    rows = heldx_ref[...] + small_dot(alpha, heldp_ref[...])
    eye = lax.broadcasted_iota(jnp.int32, rows.shape, 0) == lax.broadcasted_iota(jnp.int32, rows.shape, 1)
    held_ref[...] = jnp.sum(jnp.where(eye, rows, 0.0), axis=0, keepdims=True)


def last_step(markers, *args):
    return pl.pallas_call(
        functools.partial(last_kernel, markers),
        out_shape=[jax.ShapeDtypeStruct(args[5].shape, F32), jax.ShapeDtypeStruct((1, RHS), F32)],
        compiler_params=PARAMS,
        name="last",
    )(*args)


def on_ind(move):
    pairs = []
    for y in range(YSIZE):
        for x in range(XSIZE):
            for c in range(CORES):
                ty, tx, tc = move(y, x, c)
                pairs.append(((y * XSIZE + x) * CORES + c, (ty * XSIZE + tx) * CORES + tc))
    return pairs


def swap_cores(value):
    return lax.ppermute(value, "ind", on_ind(lambda y, x, c: (y, x, 1 - c)))


def sum_ind(value):
    value = value + swap_cores(value)
    for along in ("x", "y"):
        moved = {}
        for d in (1, 3, 2):
            if along == "x":
                pairs = on_ind(lambda y, x, c, d=d: (y, x ^ d, c))
            else:
                pairs = on_ind(lambda y, x, c, d=d: (y ^ d, x, c))
            moved[d] = lax.ppermute(value, "ind", pairs)
        value = (moved[3] + moved[1]) + (moved[2] + value)
    return value


def exchange(value):
    return lax.all_to_all(value, "snp", 0, 0)


def shards(genotypes, targets, ridge, held_out):
    rows, cols = genotypes.shape
    parts = lax.axis_size("snp")
    total = rows * lax.axis_size("ind")
    markers = cols * parts

    codes, pay, resid, lam, chosen = prep(genotypes, targets.T, held_out[None, :], ridge)
    for k in range(ITERS):
        first, last = k == 0, k == ITERS - 1
        red = sum_ind(pay)
        if first:
            u, stat, norm, pp, heldp, out = panel(total, True, False, parts, red, codes)
        else:
            *new_u, norm, pp, heldp, beta, out = panel(total, False, last, parts, red, codes, u, stat, inv, pp, heldp)
            u = new_u[0] if new_u else None
        got = exchange(out)
        if last:
            break
        args = [lam, got, pp, norm, resid, heldp]
        if first:
            direction = resid
            send, alpha, inv, heldx, sol, base = solve(markers, True, *args)
        else:
            send, alpha, inv, heldx, sol, base, direction = solve(
                markers, False, *args, heldx, beta, direction, sol)
        image = exchange(send)
        resid, pay = step(image, alpha, base, direction, codes, chosen)
    sol, held = last_step(markers, lam, got, pp, norm, beta, resid, direction, sol, heldp, heldx)
    return sol.T, held[0]


def solution(mesh):
    return jax.shard_map(
        shards,
        mesh=mesh,
        in_specs=(P("ind", "snp"), P("ind", None), P(), P()),
        out_specs=(P("ind", None), P()),
        check_vma=False,
    )
```
